512 devices in a mesh: dp: 4 (over x), seq: 64 (over y, z), tensor: 2 (over core).
Axes of the slice: x: 4, y: 8, z: 8, core: 2. Of those that a mesh axis runs over, the one named last changes fastest.
Arguments:
- q_raw: bfloat16 [4, 24576, 1536], P('dp', 'seq', 'tensor')
- k_raw: bfloat16 [4, 24576, 1536], P('dp', 'seq', 'tensor')
- values: bfloat16 [4, 24576, 1536], P('dp', 'seq', 'tensor'), may hold values from -6 to 6
- d_out: bfloat16 [4, 24576, 1536], P('dp', 'seq', 'tensor')
- gain_q: float32 [128], replicated, may hold values from 0.5 to 4.5
- gain_k: float32 [128], replicated, may hold values from 0.5 to 4.5
- tile_lists: int32 [4, 64, 3], P('dp'), may hold values from 0 to 63, as said below
- tile_counts: int32 [4, 64], P('dp'), may hold values from 1 to 3, as said below
Outputs:
- grad_q_raw: bfloat16 [4, 24576, 1536], P('dp', 'seq', 'tensor')
- grad_k_raw: bfloat16 [4, 24576, 1536], P('dp', 'seq', 'tensor')
- grad_values: bfloat16 [4, 24576, 1536], P('dp', 'seq', 'tensor')
- grad_gain_q: float32 [128], replicated
- grad_gain_k: float32 [128], replicated
The draws below stay inside these ranges and needn't reach their ends.
Inputs may be any that keep to these rules, and one draw needn't show every extreme that they name: `tile_lists`: entry 0 of row a is a itself; the next entries up to the count are distinct tiles that share a face with a in the grid of 16 x 2 x 2 tiles, where tile index = (t * 2 + h) * 2 + w; entries past the count equal a. `tile_counts`: some tile of each clip attends 3 tiles.
All inputs are finite; a program needn't handle non-finite values.
Results may differ from the reference program's by a relative error of at most 0.0085.
The reference program's roundings to bfloat16 on the way count: a program that leaves them out, or rounds other values in their place, can miss the bound.
Values may be sent and summed in bfloat16 or wider, within the bound.
A program may use at most 128 MiB of HBM per device.

```python
import math
import jax
import jax.numpy as jnp
from jax import lax

HEADS = 12
HD = 128
TILE = 384
MOST = 3
TGH = 2
TGW = 2
TGT = 16
TILES = 64
CLIPS = 4
TOKENS = 24576
FEAT = 1536


def scaled_field(noise, key):
    row_key, col_key = jax.random.split(key)
    rows_scale = jnp.exp(jax.random.uniform(row_key, (CLIPS, TOKENS, HEADS, 1), jnp.float32, 0.0, math.log(10.0)))
    cols_scale = jnp.exp(jax.random.uniform(col_key, (HD,), jnp.float32, 0.0, math.log(3.0)))
    return noise * rows_scale * cols_scale


def draw_q_raw(key, part):
    key = jax.random.fold_in(key, 2)
    noise_key, scale_key = jax.random.split(key, 2)
    shape = (CLIPS, TOKENS, HEADS, HD)
    noise = jax.random.normal(noise_key, shape, jnp.float32)
    field = scaled_field(noise, scale_key)
    return field.reshape(CLIPS, TOKENS, HEADS * HD).astype(jnp.bfloat16)


def draw_k_raw(key, part):
    key = jax.random.fold_in(key, 3)
    noise_key, scale_key = jax.random.split(key, 2)
    shape = (CLIPS, TOKENS, HEADS, HD)
    noise = jax.random.normal(noise_key, shape, jnp.float32)
    field = scaled_field(noise, scale_key)
    return field.reshape(CLIPS, TOKENS, HEADS * HD).astype(jnp.bfloat16)


def draw_d_out(key, part):
    key = jax.random.fold_in(key, 5)
    noise_key = jax.random.fold_in(key, 0)
    shape = (CLIPS, TOKENS, HEADS * HD)
    rise = 3.0 ** (jnp.arange(TOKENS, dtype=jnp.float32) / TOKENS)
    noise = jax.random.normal(noise_key, shape, jnp.float32)
    return (noise * rise[None, :, None]).astype(jnp.bfloat16)


def draw_gain_q(key, part):
    key = jax.random.fold_in(key, 11)
    gain = jax.random.uniform(key, (HD,), jnp.float32, 0.5, 2.0)
    return gain.astype(jnp.float32)


def draw_gain_k(key, part):
    key = jax.random.fold_in(key, 12)
    gain = jax.random.uniform(key, (HD,), jnp.float32, 0.5, 2.0)
    return gain.astype(jnp.float32)


def tile_plan(key):
    key = jax.random.fold_in(key, 7)
    score_key, count_key, chosen_key = jax.random.split(key, 3)
    tiles = jnp.arange(TILES, dtype=jnp.int32)
    along_t = tiles // (TGH * TGW)
    along_h = tiles // TGW % TGH
    along_w = tiles % TGW
    offsets = jnp.array([1, -1, TGW, -TGW, TGH * TGW, -TGH * TGW], jnp.int32)
    valid = jnp.stack([along_w + 1 < TGW, along_w >= 1, along_h + 1 < TGH, along_h >= 1, along_t + 1 < TGT, along_t >= 1], axis=1)
    raw = jax.random.randint(score_key, (CLIPS, TILES, 6), 0, 1000)
    ranked = jnp.where(valid[None], raw * 8 + jnp.arange(6, dtype=jnp.int32), -1)
    order = lax_top(ranked)
    neighbours = tiles[None, :, None] + offsets[order]
    available = jnp.sum(valid.astype(jnp.int32), axis=1)
    counts = jax.random.randint(count_key, (CLIPS, TILES), 1, MOST + 1)
    counts = jnp.minimum(counts, available[None] + 1)
    chosen = jax.random.randint(chosen_key, (CLIPS,), 0, TILES)
    counts = jnp.where(tiles[None] == chosen[:, None], MOST, counts).astype(jnp.int32)
    selfs = jnp.broadcast_to(tiles[None, :, None], (CLIPS, TILES, 1))
    lists = jnp.concatenate([selfs, neighbours[:, :, :MOST - 1]], axis=2)
    entries = jnp.arange(MOST, dtype=jnp.int32)
    lists = jnp.where(entries[None, None] < counts[:, :, None], lists, selfs)
    return (lists.astype(jnp.int32), counts)


def lax_top(ranked):
    return jax.lax.top_k(ranked, 6)[1]


def draw_tile_lists(key, part):
    return tile_plan(key)[0]


def draw_tile_counts(key, part):
    return tile_plan(key)[1]


def level_of(own_key, shape, cuts, least, top_value):
    factor_of = 1.0
    for axis_at, blocks in cuts:
        steps = jax.random.uniform(jax.random.fold_in(jax.random.fold_in(own_key, 6), axis_at), (blocks,), jnp.float32, least / len(cuts), top_value / len(cuts))
        factor_of = factor_of * jnp.repeat(jnp.exp(steps), shape[axis_at] // blocks).reshape((-1,) + (1,) * (len(shape) - 1 - axis_at))
    return factor_of


def scatter_about(rng, shape, width, bound, pieces=(), held_as=jnp.bfloat16):
    level = level_of(rng, shape, pieces, -0.22, 0.18) if pieces else 1.0
    values = jax.random.normal(rng, shape, jnp.float32) * width * level
    return jnp.minimum(jnp.maximum(values, -bound), bound).astype(held_as)


def setup_inputs(seed: int = 0) -> dict:
    arg_keys = jax.random.split(jax.random.key(seed), 9)
    return {
        "q_raw": draw_q_raw(jax.random.fold_in(arg_keys[8], 71), 0),
        "k_raw": draw_k_raw(jax.random.fold_in(arg_keys[8], 71), 0),
        "values": scatter_about(arg_keys[2], (CLIPS, TOKENS, FEAT), 1.0, 6.0, ((0, 4), (1, 64), (2, 2))),
        "d_out": draw_d_out(jax.random.fold_in(arg_keys[8], 71), 0),
        "gain_q": draw_gain_q(jax.random.fold_in(arg_keys[8], 71), 0),
        "gain_k": draw_gain_k(jax.random.fold_in(arg_keys[8], 71), 0),
        "tile_lists": draw_tile_lists(jax.random.fold_in(arg_keys[8], 71), 0),
        "tile_counts": draw_tile_counts(jax.random.fold_in(arg_keys[8], 71), 0),
    }


EPS = 1e-06

def normalize(raw):
    wide = raw.astype(jnp.float32).reshape(raw.shape[0], HEADS, HD)
    inverse = lax.rsqrt(lax.optimization_barrier(jnp.mean(wide * wide, axis=-1, keepdims=True)) + EPS)
    return (wide * inverse, inverse)

def norm_backward(grad, normed, inverse, gain):
    scaled = grad * gain
    inner = lax.optimization_barrier(jnp.mean(normed * scaled, axis=-1, keepdims=True))
    return ((scaled - normed * inner) * inverse, lax.optimization_barrier(jnp.sum(grad * normed, axis=(0, 1))))

def rounded(value):
    return lax.optimization_barrier(value.astype(jnp.bfloat16)).astype(jnp.float32)

def one_clip(q_raw, k_raw, values, d_out, gain_q, gain_k, lists, counts):
    factor = HD ** (-0.5)
    q_normed, q_inverse = normalize(q_raw)
    k_normed, k_inverse = normalize(k_raw)
    query = (q_normed * gain_q).astype(jnp.bfloat16).reshape(TILES, TILE, HEADS, HD)
    key = (k_normed * gain_k).astype(jnp.bfloat16).reshape(TILES, TILE, HEADS, HD)
    value = values.reshape(TILES, TILE, HEADS, HD)
    grad_out = d_out.reshape(TILES, TILE, HEADS, HD)
    entries = jnp.arange(MOST, dtype=jnp.int32)

    def per_tile(store, index):
        ids = lists[index].astype(jnp.int32)
        valid = entries < counts[index]
        q_tile = query[index].astype(jnp.float32)
        g_tile = grad_out[index].astype(jnp.float32)
        k_tiles = key[ids].astype(jnp.float32)
        v_tiles = value[ids].astype(jnp.float32)
        scores = jnp.einsum('qhd,ekhd->ehqk', q_tile, k_tiles) * factor
        scores = jnp.where(valid[:, None, None, None], scores, -jnp.inf)
        log_total = jax.nn.logsumexp(scores, axis=(0, 3))
        prob = jnp.exp(scores - log_total[None, :, :, None])
        dprob = jnp.einsum('qhd,ekhd->ehqk', g_tile, v_tiles)
        delta = lax.optimization_barrier(jnp.sum(prob * dprob, axis=(0, 3)))
        dscore = rounded(prob * (dprob - delta[None, :, :, None]))
        grad_q = factor * jnp.einsum('ehqk,ekhd->qhd', dscore, k_tiles)
        grad_k = rounded(factor * jnp.einsum('ehqk,qhd->ekhd', dscore, q_tile))
        grad_v = rounded(jnp.einsum('ehqk,qhd->ekhd', rounded(prob), g_tile))
        terms = jnp.stack([grad_k, grad_v], axis=1) * valid[:, None, None, None, None].astype(jnp.float32)
        return (store.at[ids].add(terms), grad_q)
    empty = jnp.zeros((TILES, 2, TILE, HEADS, HD), jnp.float32)
    store, grad_q_tiles = lax.scan(per_tile, empty, jnp.arange(TILES, dtype=jnp.int32))
    grad_query = grad_q_tiles.reshape(TOKENS, HEADS, HD)
    grad_key = store[:, 0].reshape(TOKENS, HEADS, HD)
    grad_q_raw, gain_part_q = norm_backward(grad_query, q_normed, q_inverse, gain_q)
    grad_k_raw, gain_part_k = norm_backward(grad_key, k_normed, k_inverse, gain_k)
    grad_values = store[:, 1].reshape(TOKENS, FEAT).astype(jnp.bfloat16)
    return (grad_q_raw.reshape(TOKENS, FEAT).astype(jnp.bfloat16), grad_k_raw.reshape(TOKENS, FEAT).astype(jnp.bfloat16), grad_values, gain_part_q, gain_part_k)

def reference(q_raw, k_raw, values, d_out, gain_q, gain_k, tile_lists, tile_counts):
    grads_q, grads_k, grads_v = ([], [], [])
    total_q = jnp.zeros((HD,), jnp.float32)
    total_k = jnp.zeros((HD,), jnp.float32)
    for clip in range(CLIPS):
        result = one_clip(q_raw[clip], k_raw[clip], values[clip], d_out[clip], gain_q, gain_k, tile_lists[clip], tile_counts[clip])
        grads_q.append(result[0])
        grads_k.append(result[1])
        grads_v.append(result[2])
        total_q = total_q + result[3]
        total_k = total_k + result[4]
    factor = (CLIPS * TOKENS) ** (-0.5)
    return (jnp.stack(grads_q), jnp.stack(grads_k), jnp.stack(grads_v), total_q * factor, total_k * factor)
```

```python
import functools

import jax
import jax.numpy as jnp
from jax import lax
from jax.experimental import pallas as pl
from jax.experimental.pallas import tpu as pltpu
from jax.sharding import PartitionSpec as P

MESH = pl.DeviceIdType.MESH
EPS = 1e-06
LOG2E = 1.4426950408889634
FAR = 1e30
ROWS = 384
HD = 128
HEADS_HERE = 6
BLOCK = 128
RING = 8
NEAR = 4
F32 = jnp.float32
BF16 = jnp.bfloat16


def flip(z, mask):
    result = z
    for bit in (1, 2, 4):
        if mask & bit:
            result = result + bit - 2 * bit * ((z // bit) % 2)
    return result


def dot_t(a, b):
    return lax.dot_general(a, b, (((1,), (1,)), ((), ())), preferred_element_type=F32)


def dot(a, b):
    return lax.dot_general(a, b, (((1,), (0,)), ((), ())), preferred_element_type=F32)


def inverse_norm(wide):
    return lax.rsqrt(jnp.mean(wide * wide, axis=-1, keepdims=True) + EPS)


def stacked(rows):
    place = lax.broadcasted_iota(jnp.int32, (8, rows[0].shape[-1]), 0)
    out = jnp.broadcast_to(rows[-1], place.shape)
    for index in range(len(rows) - 2, -1, -1):
        out = jnp.where(place == index, rows[index], out)
    return out


def attention_kernel(
    lists, counts, q_ref, k_ref, v_ref, g_ref, gain_q_ref, gain_k_ref,
    dq_ref, dk_ref, dv_ref, gain_ref,
    slots, keys, key_t, part_out, part_in, final_out, final_in, dq32, dq_out, ret_in, ds_ref, dk_acc, dv_acc,
    slot_send, slot_recv, part_send, part_recv, final_send, final_recv, ret_send, ret_recv,
):
    factor = HD ** (-0.5)
    scale2 = factor * LOG2E
    mine = lax.axis_index("seq")
    y, z = mine // RING, mine % RING
    late = z // 4
    y_next = (y + 1 - 2 * late + RING) % RING
    y_prev = (y - 1 + 2 * late + RING) % RING
    along_w = y * RING + flip(z, 1)
    along_h = y * RING + flip(z, 2)
    relay = y * RING + flip(z, 6)
    along_t = y * RING + flip(z, 4)
    along_u = y_prev * RING + flip(z, 4)
    below = y_next * RING + z
    above = y_prev * RING + z
    owners = (along_w, along_h, along_t, along_u)

    barrier = pltpu.get_barrier_semaphore()
    for partner in (along_w, along_h, relay, along_t, along_u, below, above):
        pl.semaphore_signal(barrier, inc=1, device_id={"seq": partner}, device_id_type=MESH)

    def lanes(h):
        return pl.ds(pl.multiple_of(h * HD, HD), HD)

    def prepare_q(h, carry):
        wide = q_ref[:, lanes(h)].astype(F32)
        slots[0, h, 0] = (wide * inverse_norm(wide) * gain_q_ref[...]).astype(BF16)
        slots[0, h, 1] = g_ref[:, lanes(h)]
        return carry

    def prepare_k(h, carry):
        wide = k_ref[:, lanes(h)].astype(F32)
        key = (wide * inverse_norm(wide) * gain_k_ref[...]).astype(BF16)
        keys[h, 0] = key
        keys[h, 1] = v_ref[:, lanes(h)]
        key_t[h] = key.astype(F32).T.astype(BF16)
        return carry

    def remote(src, dst, send, recv, target):
        return pltpu.make_async_remote_copy(
            src_ref=src, dst_ref=dst, send_sem=send, recv_sem=recv, device_id={"seq": target}, device_id_type=MESH
        )

    def fetch(source, place, h, target):
        return remote(slots.at[source, h], slots.at[place, h], slot_send.at[place - 1, h], slot_recv.at[place - 1, h], target)

    def to_w(h):
        return fetch(0, 1, h, along_w)

    def to_h(h):
        return fetch(0, 2, h, along_h)

    def to_relay(h):
        return fetch(2, 3, h, relay)

    def to_y(h):
        return fetch(3, 4, h, below)

    def part_copy(place, h):
        return remote(
            part_out.at[place, h], part_in.at[place, h], part_send.at[place, h], part_recv.at[place, h], owners[place - 1]
        )

    def final_copy(place, h):
        return remote(
            final_out.at[place, h], final_in.at[place, h], final_send.at[place, h], final_recv.at[place, h], owners[place - 1]
        )

    def ret_copy(place, h, target):
        return remote(
            dq_out.at[place, h], ret_in.at[place, h], ret_send.at[place, h], ret_recv.at[place, h], target
        )

    def ret_w(h):
        return ret_copy(0, h, along_w)

    def ret_h(h):
        return ret_copy(1, h, along_h)

    def ret_relay(h):
        return ret_copy(2, h, relay)

    def ret_y(h):
        return ret_copy(3, h, above)

    flags = []
    for owner in owners:
        hit = jnp.int32(0)
        for entry in range(1, 3):
            same = jnp.where(lists[mine, entry] == owner, 1, 0)
            hit = hit + jnp.where(entry < counts[mine], same, 0)
        flags.append(hit > 0)

    def stats(place, h):
        query, grad = slots[place, h, 0], slots[place, h, 1]
        top = total = inner = None
        for block in range(ROWS // BLOCK):
            rows = pl.ds(block * BLOCK, BLOCK)
            scores = dot_t(keys[h, 0, rows], query) * scale2
            dprob = dot_t(keys[h, 1, rows], grad)
            high = jnp.max(scores, axis=0, keepdims=True)
            new_top = high if top is None else jnp.maximum(top, high)
            weight = jnp.exp2(scores - new_top)
            new_total = jnp.sum(weight, axis=0, keepdims=True)
            new_inner = jnp.sum(weight * dprob, axis=0, keepdims=True)
            if top is not None:
                keep = jnp.exp2(top - new_top)
                new_total = new_total + total * keep
                new_inner = new_inner + inner * keep
            top, total, inner = new_top, new_total, new_inner
        part_out[place, h] = stacked((top, total, inner))

    def combine(h):
        parts = [part_out[0, h]] + [part_in[n + 1, h] for n in range(NEAR)]
        tops = [parts[0][0:1]] + [jnp.where(flags[n], parts[n + 1][0:1], -FAR) for n in range(NEAR)]
        top = functools.reduce(jnp.maximum, tops)
        weights = [jnp.exp2(t - top) for t in tops]
        total = sum(p[1:2] * w for p, w in zip(parts, weights))
        inner = sum(p[2:3] * w for p, w in zip(parts, weights))
        log_total = top + jnp.log(total) * LOG2E
        delta = inner / total
        final_in[0, h] = stacked((log_total, delta))
        for n in range(NEAR):
            final_out[n + 1, h] = stacked((jnp.where(flags[n], log_total, FAR), delta))

    def grads(place, h):
        query, grad = slots[place, h, 0], slots[place, h, 1]
        final = final_in[place, h]
        log_total, delta = final[0:1], final[1:2]
        for block in range(ROWS // BLOCK):
            rows = pl.ds(block * BLOCK, BLOCK)
            scores = dot_t(keys[h, 0, rows], query) * scale2
            dprob = dot_t(keys[h, 1, rows], grad)
            prob = jnp.exp2(scores - log_total)
            dscore = (prob * (dprob - delta)).astype(BF16)
            ds_ref[rows] = dscore
            dv_acc[rows] += dot(prob.astype(BF16), grad)
            dk_acc[rows] += dot(dscore, query)
        dq32[place, h] = dot(key_t[h], ds_ref[...]) * factor

    def norm_backward(grad, raw, gain):
        wide = raw.astype(F32)
        inverse = inverse_norm(wide)
        normed = wide * inverse
        scaled = grad * gain
        mean = jnp.mean(normed * scaled, axis=-1, keepdims=True)
        return ((scaled - normed * mean) * inverse).astype(BF16), jnp.sum(grad * normed, axis=0, keepdims=True)

    def backward(h):
        dk_acc[...] = jnp.zeros_like(dk_acc)
        dv_acc[...] = jnp.zeros_like(dv_acc)
        lax.fori_loop(0, NEAR + 1, lambda place, carry: (grads(place, h), carry)[1], 0)
        dq_out[0, h] = dq32[1, h].astype(BF16)
        dq_out[3, h] = dq32[4, h].astype(BF16)

    def finish_k(h):
        dv_ref[:, lanes(h)] = dv_acc[...].astype(BF16)
        grad, gain = norm_backward(dk_acc[...] * factor, k_ref[:, lanes(h)], gain_k_ref[...])
        dk_ref[:, lanes(h)] = grad
        gain_ref[1:2] += gain

    def finish_q(h):
        total = dq32[0, h] + ret_in[0, h].astype(F32) + ret_in[1, h].astype(F32)
        grad, gain = norm_backward(total.T, q_ref[:, lanes(h)], gain_q_ref[...])
        dq_ref[:, lanes(h)] = grad
        gain_ref[0:1] += gain

    gain_ref[...] = jnp.zeros_like(gain_ref)
    lax.fori_loop(0, HEADS_HERE, prepare_q, 0)
    pl.semaphore_wait(barrier, 7)
    to_h(0).start()
    to_h(1).start()
    to_w(0).start()
    lax.fori_loop(0, HEADS_HERE, prepare_k, 0)

    def step(i, carry):
        def on(lag, stage):
            h = i - lag

            @pl.when(jnp.logical_and(h >= 0, h < HEADS_HERE))
            def _():
                stage(h)

        def arrive(h):
            to_h(h).wait_recv()
            to_relay(h).start()

            @pl.when(h + 2 < HEADS_HERE)
            def _():
                to_h(h + 2).start()

            @pl.when(h + 1 < HEADS_HERE)
            def _():
                to_w(h + 1).start()

            stats(0, h)
            stats(2, h)

        def pass_on(h):
            to_relay(h).wait_recv()
            to_y(h).start()

        def near_w(h):
            to_w(h).wait_recv()
            stats(1, h)

        def send_parts(h):
            to_y(h).wait_recv()
            stats(4, h)
            for place in range(1, NEAR + 1):
                part_copy(place, h).start()

        def pairs(h):
            for place in range(1, NEAR + 1):
                final_copy(place, h).wait_recv()
            backward(h)
            ret_w(h).start()
            ret_y(h).start()
            finish_k(h)

        def send_finals(h):
            for place in range(1, NEAR + 1):
                part_copy(place, h).wait_recv()
            combine(h)
            for place in range(1, NEAR + 1):
                final_copy(place, h).start()

        def back_y(h):
            ret_y(h).wait_recv()
            dq_out[2, h] = (dq32[3, h] + ret_in[3, h].astype(F32)).astype(BF16)
            ret_relay(h).start()

        def back_relay(h):
            ret_relay(h).wait_recv()
            dq_out[1, h] = (dq32[2, h] + ret_in[2, h].astype(F32)).astype(BF16)
            ret_h(h).start()

        def back_home(h):
            ret_w(h).wait_recv()
            ret_h(h).wait_recv()
            finish_q(h)

        on(0, arrive)
        on(1, pass_on)
        on(0, near_w)
        on(1, lambda h: stats(3, h))
        on(2, send_parts)
        on(3, pairs)
        on(2, send_finals)
        on(4, back_y)
        on(5, back_relay)
        on(6, back_home)
        return carry

    lax.fori_loop(0, HEADS_HERE + 6, step, 0)

    def drain(h, carry):
        for copy in (to_w, to_h, to_relay, to_y, ret_w, ret_h, ret_relay, ret_y):
            copy(h).wait_send()
        for place in range(1, NEAR + 1):
            part_copy(place, h).wait_send()
            final_copy(place, h).wait_send()
        return carry

    lax.fori_loop(0, HEADS_HERE, drain, 0)


def attention(lists, counts, q, k, v, g, gain_q, gain_k):
    n = HEADS_HERE
    vmem = pl.BlockSpec(memory_space=pltpu.VMEM)
    smem = pl.BlockSpec(memory_space=pltpu.SMEM)
    big = jax.ShapeDtypeStruct((ROWS, n * HD), BF16)
    sem = pltpu.SemaphoreType.DMA
    return pl.pallas_call(
        attention_kernel,
        name="tile_attention",
        out_shape=(big, big, big, jax.ShapeDtypeStruct((8, HD), F32)),
        in_specs=[smem, smem] + [vmem] * 6,
        out_specs=(vmem,) * 4,
        scratch_shapes=[
            pltpu.VMEM((5, n, 2, ROWS, HD), BF16),
            pltpu.VMEM((n, 2, ROWS, HD), BF16),
            pltpu.VMEM((n, HD, ROWS), BF16),
            pltpu.VMEM((5, n, 8, ROWS), F32),
            pltpu.VMEM((5, n, 8, ROWS), F32),
            pltpu.VMEM((5, n, 8, ROWS), F32),
            pltpu.VMEM((5, n, 8, ROWS), F32),
            pltpu.VMEM((5, n, HD, ROWS), F32),
            pltpu.VMEM((4, n, HD, ROWS), BF16),
            pltpu.VMEM((4, n, HD, ROWS), BF16),
            pltpu.VMEM((ROWS, ROWS), BF16),
            pltpu.VMEM((ROWS, HD), F32),
            pltpu.VMEM((ROWS, HD), F32),
            sem((4, n)), sem((4, n)), sem((5, n)), sem((5, n)), sem((5, n)), sem((5, n)), sem((4, n)), sem((4, n)),
        ],
        compiler_params=pltpu.CompilerParams(collective_id=1, has_side_effects=True, vmem_limit_bytes=56 * 2**20),
    )(lists, counts, q, k, v, g, gain_q, gain_k)


def total_kernel(part_ref, out_ref, held_a, held_b, held_c, sends, recvs):
    x, s, c = lax.axis_index("dp"), lax.axis_index("seq"), lax.axis_index("tensor")
    y, z = s // RING, s % RING
    groups = (
        (held_a, x * 2 + c, lambda p: {"dp": p // 2, "tensor": p % 2}),
        (held_b, y, lambda p: {"seq": p * RING + z}),
        (held_c, z, lambda p: {"seq": y * RING + p}),
    )
    barrier = pltpu.get_barrier_semaphore()
    for _, me, where in groups:
        for step in range(1, 8):
            pl.semaphore_signal(barrier, inc=1, device_id=where((me + step) % 8), device_id_type=MESH)
    value = part_ref[...]
    pl.semaphore_wait(barrier, 21)
    for g, (held, me, where) in enumerate(groups):
        held[me] = value

        def copy(step):
            return pltpu.make_async_remote_copy(
                src_ref=held.at[me], dst_ref=held.at[me], send_sem=sends.at[g, step], recv_sem=recvs.at[g, step],
                device_id=where((me + step) % 8), device_id_type=MESH,
            )

        copies = [copy(step) for step in range(1, 8)]
        for item in copies:
            item.start()
        for item in copies:
            item.wait_recv()
        for item in copies:
            item.wait_send()
        value = held[0]
        for place in range(1, 8):
            value = value + held[place]
    out_ref[...] = value


def total(part):
    vmem = pl.BlockSpec(memory_space=pltpu.VMEM)
    sem = pltpu.SemaphoreType.DMA
    return pl.pallas_call(
        total_kernel,
        name="gain_total",
        out_shape=jax.ShapeDtypeStruct((8, HD), F32),
        in_specs=[vmem],
        out_specs=vmem,
        scratch_shapes=[pltpu.VMEM((8, 8, HD), F32)] * 3 + [sem((3, 8)), sem((3, 8))],
        compiler_params=pltpu.CompilerParams(collective_id=2, has_side_effects=True),
    )(part)


def shards(q_raw, k_raw, values, d_out, gain_q, gain_k, tile_lists, tile_counts):
    grad_q, grad_k, grad_v, gains = attention(
        tile_lists[0], tile_counts[0], q_raw[0], k_raw[0], values[0], d_out[0], gain_q[None], gain_k[None]
    )
    gains = total(gains)
    scale_back = (lax.axis_size("dp") * lax.axis_size("seq") * ROWS) ** (-0.5)
    return (grad_q[None], grad_k[None], grad_v[None], gains[0] * scale_back, gains[1] * scale_back)


def solution(mesh):
    split = P("dp", "seq", "tensor")
    return jax.shard_map(
        shards,
        mesh=mesh,
        in_specs=(split, split, split, split, P(), P(), P("dp", None, None), P("dp", None)),
        out_specs=(split, split, split, P(), P()),
        check_vma=False,
    )
```

```python
import functools

import jax
import jax.numpy as jnp
from jax import lax
from jax.experimental import pallas as pl
from jax.experimental.pallas import tpu as pltpu
from jax.sharding import PartitionSpec as P

MESH = pl.DeviceIdType.MESH
EPS = 1e-06
LOG2E = 1.4426950408889634
FAR = 1e30
ROWS = 384
HD = 128
HEADS_HERE = 6
BLOCK = 128
RING = 8
NEAR = 4
F32 = jnp.float32
BF16 = jnp.bfloat16


def flip(z, mask):
    result = z
    for bit in (1, 2, 4):
        if mask & bit:
            result = result + bit - 2 * bit * ((z // bit) % 2)
    return result


def dot_t(a, b):
    return lax.dot_general(a, b, (((1,), (1,)), ((), ())), preferred_element_type=F32)


def dot(a, b):
    return lax.dot_general(a, b, (((1,), (0,)), ((), ())), preferred_element_type=F32)


def inverse_norm(wide):
    return lax.rsqrt(jnp.mean(wide * wide, axis=-1, keepdims=True) + EPS)


def stacked(first, second):
    place = lax.broadcasted_iota(jnp.int32, (2, first.shape[-1]), 0)
    return jnp.where(place == 0, first, second)


def attention_kernel(
    lists, counts, q_ref, k_ref, v_ref, g_ref, gain_q_ref, gain_k_ref,
    dq_ref, dk_ref, dv_ref, gain_out_ref,
    slots, keys, key_t, part_out, part_in, final_out, final_in, dq32, dq_out, ret_in, ds_ref, dk_acc, dv_acc,
    gain_ref, gain_a, gain_b, gain_c,
    slot_send, slot_recv, part_send, part_recv, final_send, final_recv, ret_send, ret_recv, gain_send, gain_recv,
):
    factor = HD ** (-0.5)
    scale2 = factor * LOG2E
    mine = lax.axis_index("seq")
    y, z = mine // RING, mine % RING
    late = z // 4
    y_next = (y + 1 - 2 * late + RING) % RING
    y_prev = (y - 1 + 2 * late + RING) % RING
    along_w = y * RING + flip(z, 1)
    along_h = y * RING + flip(z, 2)
    relay = y * RING + flip(z, 6)
    along_t = y * RING + flip(z, 4)
    along_u = y_prev * RING + flip(z, 4)
    below = y_next * RING + z
    above = y_prev * RING + z
    owners = (along_w, along_h, along_t, along_u)

    barrier = pltpu.get_barrier_semaphore()
    for partner in (along_w, along_h, relay, along_t, along_u, below, above):
        pl.semaphore_signal(barrier, inc=1, device_id={"seq": partner}, device_id_type=MESH)
    clip, core = lax.axis_index("dp"), lax.axis_index("tensor")
    groups = (
        (gain_a, clip * 2 + core, lambda p: {"dp": p // 2, "tensor": p % 2}),
        (gain_b, y, lambda p: {"seq": p * RING + z}),
        (gain_c, z, lambda p: {"seq": y * RING + p}),
    )
    for _, me, where in groups:
        for hop in range(1, RING):
            pl.semaphore_signal(barrier, inc=1, device_id=where((me + hop) % RING), device_id_type=MESH)

    def lanes(h):
        return pl.ds(pl.multiple_of(h * HD, HD), HD)

    def prepare_q(h, carry):
        wide = q_ref[:, lanes(h)].astype(F32)
        slots[0, h, 0] = (wide * inverse_norm(wide) * gain_q_ref[...]).astype(BF16)
        slots[0, h, 1] = g_ref[:, lanes(h)]
        return carry

    def prepare_k(h, carry):
        wide = k_ref[:, lanes(h)].astype(F32)
        key = (wide * inverse_norm(wide) * gain_k_ref[...]).astype(BF16)
        keys[h, 0] = key
        keys[h, 1] = v_ref[:, lanes(h)]
        key_t[h] = key.astype(F32).T.astype(BF16)
        return carry

    def remote(src, dst, send, recv, target):
        return pltpu.make_async_remote_copy(
            src_ref=src, dst_ref=dst, send_sem=send, recv_sem=recv, device_id={"seq": target}, device_id_type=MESH
        )

    def fetch(source, place, h, target):
        return remote(slots.at[source, h], slots.at[place, h], slot_send.at[place - 1, h], slot_recv.at[place - 1, h], target)

    def to_w(h):
        return fetch(0, 1, h, along_w)

    def to_h(h):
        return fetch(0, 2, h, along_h)

    def to_relay(h):
        return fetch(2, 3, h, relay)

    def to_y(h):
        return fetch(3, 4, h, below)

    def part_copy(place, h):
        return remote(
            part_out.at[place, h], part_in.at[place, h], part_send.at[place, h], part_recv.at[place, h], owners[place - 1]
        )

    def final_copy(place, h):
        return remote(
            final_out.at[place, h], final_in.at[place, h], final_send.at[place, h], final_recv.at[place, h], owners[place - 1]
        )

    def ret_copy(place, h, target):
        return remote(
            dq_out.at[place, h], ret_in.at[place, h], ret_send.at[place, h], ret_recv.at[place, h], target
        )

    def ret_w(h):
        return ret_copy(0, h, along_w)

    def ret_h(h):
        return ret_copy(1, h, along_h)

    def ret_relay(h):
        return ret_copy(2, h, relay)

    def ret_y(h):
        return ret_copy(3, h, above)

    flags = []
    for owner in owners:
        hit = jnp.int32(0)
        for entry in range(1, 3):
            same = jnp.where(lists[mine, entry] == owner, 1, 0)
            hit = hit + jnp.where(entry < counts[mine], same, 0)
        flags.append(hit > 0)

    def stats(place, h):
        query, grad = slots[place, h, 0], slots[place, h, 1]
        top = total = inner = None
        for block in range(ROWS // BLOCK):
            rows = pl.ds(block * BLOCK, BLOCK)
            scores = dot_t(keys[h, 0, rows], query) * scale2
            dprob = dot_t(keys[h, 1, rows], grad)
            high = jnp.max(scores, axis=0, keepdims=True)
            new_top = high if top is None else jnp.maximum(top, high)
            weight = jnp.exp2(scores - new_top)
            new_total = jnp.sum(weight, axis=0, keepdims=True)
            new_inner = jnp.sum(weight * dprob, axis=0, keepdims=True)
            if top is not None:
                keep = jnp.exp2(top - new_top)
                new_total = new_total + total * keep
                new_inner = new_inner + inner * keep
            top, total, inner = new_top, new_total, new_inner
        part_out[place, h] = stacked(top + jnp.log(total) * LOG2E, inner / total)

    def combine(h):
        parts = [part_out[0, h]] + [part_in[n + 1, h] for n in range(NEAR)]
        tops = [parts[0][0:1]] + [jnp.where(flags[n], parts[n + 1][0:1], -FAR) for n in range(NEAR)]
        top = functools.reduce(jnp.maximum, tops)
        weights = [jnp.exp2(t - top) for t in tops]
        total = sum(weights)
        log_total = top + jnp.log(total) * LOG2E
        delta = sum(p[1:2] * w for p, w in zip(parts, weights)) / total
        final_in[0, h] = stacked(log_total, delta)
        for n in range(NEAR):
            final_out[n + 1, h] = stacked(jnp.where(flags[n], log_total, FAR), delta)

    def grads(place, h):
        query, grad = slots[place, h, 0], slots[place, h, 1]
        final = final_in[place, h]
        log_total, delta = final[0:1], final[1:2]
        for block in range(ROWS // BLOCK):
            rows = pl.ds(block * BLOCK, BLOCK)
            scores = dot_t(keys[h, 0, rows], query) * scale2
            dprob = dot_t(keys[h, 1, rows], grad)
            prob = jnp.exp2(scores - log_total)
            dscore = (prob * (dprob - delta)).astype(BF16)
            ds_ref[rows] = dscore
            dv_acc[rows] += dot(prob.astype(BF16), grad)
            dk_acc[rows] += dot(dscore, query)
        dq32[place, h] = dot(key_t[h], ds_ref[...]) * factor

    def norm_backward(grad, raw, gain):
        wide = raw.astype(F32)
        inverse = inverse_norm(wide)
        normed = wide * inverse
        scaled = grad * gain
        mean = jnp.mean(normed * scaled, axis=-1, keepdims=True)
        return ((scaled - normed * mean) * inverse).astype(BF16), jnp.sum(grad * normed, axis=0, keepdims=True)

    def backward(h):
        dk_acc[...] = jnp.zeros_like(dk_acc)
        dv_acc[...] = jnp.zeros_like(dv_acc)
        lax.fori_loop(0, NEAR + 1, lambda place, carry: (grads(place, h), carry)[1], 0)
        dq_out[0, h] = dq32[1, h].astype(BF16)
        dq_out[3, h] = dq32[4, h].astype(BF16)

    def finish_k(h):
        dv_ref[:, lanes(h)] = dv_acc[...].astype(BF16)
        grad_key = dk_acc[...] * factor
        grad, gain = norm_backward(grad_key, k_ref[:, lanes(h)], gain_k_ref[...])
        dk_ref[:, lanes(h)] = grad
        paired = jnp.sum(grad_key * keys[h, 0].astype(F32), axis=0, keepdims=True) / gain_q_ref[...]
        gain_ref[...] += stacked(paired, gain)

    def finish_q(h):
        total = dq32[0, h] + ret_in[0, h].astype(F32) + ret_in[1, h].astype(F32)
        grad, _ = norm_backward(total.T, q_ref[:, lanes(h)], gain_q_ref[...])
        dq_ref[:, lanes(h)] = grad

    def gain_copies(g):
        held, me, where = groups[g]
        return [
            pltpu.make_async_remote_copy(
                src_ref=held.at[me], dst_ref=held.at[me], send_sem=gain_send.at[g, hop], recv_sem=gain_recv.at[g, hop],
                device_id=where((me + hop) % RING), device_id_type=MESH,
            )
            for hop in range(1, RING)
        ]

    def gain_start(g, value):
        held, me, _ = groups[g]
        held[me] = value
        for copy in gain_copies(g):
            copy.start()

    def gain_finish(g):
        held, _, _ = groups[g]
        for copy in gain_copies(g):
            copy.wait_recv()
        value = held[0]
        for place in range(1, RING):
            value = value + held[place]
        return value

    gain_ref[...] = jnp.zeros_like(gain_ref)
    lax.fori_loop(0, HEADS_HERE, prepare_q, 0)
    pl.semaphore_wait(barrier, 7 + 3 * (RING - 1))
    to_h(0).start()
    to_w(0).start()
    to_h(1).start()
    to_h(2).start()
    lax.fori_loop(0, HEADS_HERE, prepare_k, 0)

    last = HEADS_HERE + 3

    def step(i, carry):
        def on(lag, stage):
            h = i - lag

            @pl.when(jnp.logical_and(h >= 0, h < HEADS_HERE))
            def _():
                stage(h)

        def arrive(h):
            to_h(h).wait_recv()
            to_relay(h).start()

            @pl.when(h + 3 < HEADS_HERE)
            def _():
                to_h(h + 3).start()

            @pl.when(h + 1 < HEADS_HERE)
            def _():
                to_w(h + 1).start()

            stats(0, h)
            stats(2, h)

        def pass_on(h):
            to_relay(h).wait_recv()
            to_y(h).start()

        def near_w(h):
            to_w(h).wait_recv()
            stats(1, h)

        def send_parts(h):
            to_y(h).wait_recv()
            stats(4, h)
            for place in range(1, NEAR + 1):
                part_copy(place, h).start()

        def pairs(h):
            for place in range(1, NEAR + 1):
                final_copy(place, h).wait_recv()
            backward(h)
            ret_w(h).start()
            ret_y(h).start()
            finish_k(h)

        def send_finals(h):
            for place in range(1, NEAR + 1):
                part_copy(place, h).wait_recv()
            combine(h)
            for place in range(1, NEAR + 1):
                final_copy(place, h).start()

        def back_y(h):
            ret_y(h).wait_recv()
            dq_out[2, h] = (dq32[3, h] + ret_in[3, h].astype(F32)).astype(BF16)
            ret_relay(h).start()

        def back_relay(h):
            ret_relay(h).wait_recv()
            dq_out[1, h] = (dq32[2, h] + ret_in[2, h].astype(F32)).astype(BF16)
            ret_h(h).start()

        def back_home(h):
            ret_w(h).wait_recv()
            ret_h(h).wait_recv()
            finish_q(h)

        on(0, arrive)
        on(1, pass_on)
        on(0, near_w)
        on(1, lambda h: stats(3, h))
        on(2, send_parts)
        on(3, send_finals)
        on(4, pairs)
        pl.when(i == last)(lambda: gain_start(0, gain_ref[...]))
        on(5, back_y)
        on(6, back_relay)
        on(7, back_home)
        pl.when(i == last + 1)(lambda: gain_start(1, gain_finish(0)))
        pl.when(i == last + 2)(lambda: gain_start(2, gain_finish(1)))
        return carry

    lax.fori_loop(0, HEADS_HERE + 7, step, 0)
    gain_out_ref[...] = gain_finish(2) * (4 * 64 * ROWS) ** (-0.5)

    def drain(h, carry):
        for copy in (to_w, to_h, to_relay, to_y, ret_w, ret_h, ret_relay, ret_y):
            copy(h).wait_send()
        for place in range(1, NEAR + 1):
            part_copy(place, h).wait_send()
            final_copy(place, h).wait_send()
        return carry

    lax.fori_loop(0, HEADS_HERE, drain, 0)
    for g in range(3):
        for copy in gain_copies(g):
            copy.wait_send()


def attention(lists, counts, q, k, v, g, gain_q, gain_k):
    n = HEADS_HERE
    vmem = pl.BlockSpec(memory_space=pltpu.VMEM)
    smem = pl.BlockSpec(memory_space=pltpu.SMEM)
    big = jax.ShapeDtypeStruct((ROWS, n * HD), BF16)
    sem = pltpu.SemaphoreType.DMA
    return pl.pallas_call(
        attention_kernel,
        name="tile_attention",
        out_shape=(big, big, big, jax.ShapeDtypeStruct((2, HD), F32)),
        in_specs=[smem, smem] + [vmem] * 6,
        out_specs=(vmem,) * 4,
        scratch_shapes=[
            pltpu.VMEM((5, n, 2, ROWS, HD), BF16),
            pltpu.VMEM((n, 2, ROWS, HD), BF16),
            pltpu.VMEM((n, HD, ROWS), BF16),
            pltpu.VMEM((5, n, 2, ROWS), F32),
            pltpu.VMEM((5, n, 2, ROWS), F32),
            pltpu.VMEM((5, n, 2, ROWS), F32),
            pltpu.VMEM((5, n, 2, ROWS), F32),
            pltpu.VMEM((5, n, HD, ROWS), F32),
            pltpu.VMEM((4, n, HD, ROWS), BF16),
            pltpu.VMEM((4, n, HD, ROWS), BF16),
            pltpu.VMEM((ROWS, ROWS), BF16),
            pltpu.VMEM((ROWS, HD), F32),
            pltpu.VMEM((ROWS, HD), F32),
            pltpu.VMEM((2, HD), F32),
            pltpu.VMEM((RING, 2, HD), F32),
            pltpu.VMEM((RING, 2, HD), F32),
            pltpu.VMEM((RING, 2, HD), F32),
            sem((4, n)), sem((4, n)), sem((5, n)), sem((5, n)), sem((5, n)), sem((5, n)), sem((4, n)), sem((4, n)),
            sem((3, RING)), sem((3, RING)),
        ],
        compiler_params=pltpu.CompilerParams(collective_id=1, has_side_effects=True, vmem_limit_bytes=56 * 2**20),
    )(lists, counts, q, k, v, g, gain_q, gain_k)


def shards(q_raw, k_raw, values, d_out, gain_q, gain_k, tile_lists, tile_counts):
    grad_q, grad_k, grad_v, gains = attention(
        tile_lists[0], tile_counts[0], q_raw[0], k_raw[0], values[0], d_out[0], gain_q[None], gain_k[None]
    )
    return (grad_q[None], grad_k[None], grad_v[None], gains[0], gains[1])


def solution(mesh):
    split = P("dp", "seq", "tensor")
    return jax.shard_map(
        shards,
        mesh=mesh,
        in_specs=(split, split, split, split, P(), P(), P("dp", None, None), P("dp", None)),
        out_specs=(split, split, split, P(), P()),
        check_vma=False,
    )
```

```python
import functools

import jax
import jax.numpy as jnp
from jax import lax
from jax.experimental import pallas as pl
from jax.experimental.pallas import tpu as pltpu
from jax.sharding import PartitionSpec as P

MESH = pl.DeviceIdType.MESH
EPS = 1e-06
LOG2E = 1.4426950408889634
FAR = 1e30
ROWS = 384
HD = 128
HEADS_HERE = 6
BLOCK = 128
RING = 8
NEAR = 4
F32 = jnp.float32
BF16 = jnp.bfloat16


def flip(z, mask):
    result = z
    for bit in (1, 2, 4):
        if mask & bit:
            result = result + bit - 2 * bit * ((z // bit) % 2)
    return result


def dot_t(a, b):
    return lax.dot_general(a, b, (((1,), (1,)), ((), ())), preferred_element_type=F32)


def dot(a, b):
    return lax.dot_general(a, b, (((1,), (0,)), ((), ())), preferred_element_type=F32)


def inverse_norm(wide):
    return lax.rsqrt(jnp.mean(wide * wide, axis=-1, keepdims=True) + EPS)


def stacked(first, second):
    place = lax.broadcasted_iota(jnp.int32, (2, first.shape[-1]), 0)
    return jnp.where(place == 0, first, second)


def attention_kernel(
    lists, counts, q_ref, k_ref, v_ref, g_ref, gain_q_ref, gain_k_ref,
    grads_ref, gain_q_out, gain_k_out,
    slots, keys, key_t, part_out, part_in, final_out, final_in, dq32, dq_out, ret_in, ds_ref, dk_acc, dv_acc,
    gain_ref, gain_a, gain_b, gain_c,
    slot_send, slot_recv, part_send, part_recv, final_send, final_recv, ret_send, ret_recv, gain_send, gain_recv,
):
    factor = HD ** (-0.5)
    scale2 = factor * LOG2E
    mine = lax.axis_index("seq")
    y, z = mine // RING, mine % RING
    late = z // 4
    y_next = (y + 1 - 2 * late + RING) % RING
    y_prev = (y - 1 + 2 * late + RING) % RING
    along_w = y * RING + flip(z, 1)
    along_h = y * RING + flip(z, 2)
    relay = y * RING + flip(z, 6)
    along_t = y * RING + flip(z, 4)
    along_u = y_prev * RING + flip(z, 4)
    below = y_next * RING + z
    above = y_prev * RING + z
    owners = (along_w, along_h, along_t, along_u)

    barrier = pltpu.get_barrier_semaphore()
    for partner in (along_w, along_h, relay, along_t, along_u, below, above):
        pl.semaphore_signal(barrier, inc=1, device_id={"seq": partner}, device_id_type=MESH)
    clip, core = lax.axis_index("dp"), lax.axis_index("tensor")
    groups = (
        (gain_a, clip * 2 + core, lambda p: {"dp": p // 2, "tensor": p % 2}),
        (gain_b, y, lambda p: {"seq": p * RING + z}),
        (gain_c, z, lambda p: {"seq": y * RING + p}),
    )
    for _, me, where in groups:
        for hop in range(1, RING):
            pl.semaphore_signal(barrier, inc=1, device_id=where((me + hop) % RING), device_id_type=MESH)

    def lanes(h):
        return pl.ds(pl.multiple_of(h * HD, HD), HD)

    def prepare_q(h, carry):
        wide = q_ref[:, lanes(h)].astype(F32)
        slots[0, h, 0] = (wide * inverse_norm(wide) * gain_q_ref[...]).astype(BF16)
        slots[0, h, 1] = g_ref[:, lanes(h)]
        return carry

    def prepare_k(h, carry):
        wide = k_ref[:, lanes(h)].astype(F32)
        key = (wide * inverse_norm(wide) * gain_k_ref[...]).astype(BF16)
        keys[h, 0] = key
        keys[h, 1] = v_ref[:, lanes(h)]
        key_t[h] = key.astype(F32).T.astype(BF16)
        return carry

    def remote(src, dst, send, recv, target):
        return pltpu.make_async_remote_copy(
            src_ref=src, dst_ref=dst, send_sem=send, recv_sem=recv, device_id={"seq": target}, device_id_type=MESH
        )

    def fetch(source, place, h, target):
        return remote(slots.at[source, h], slots.at[place, h], slot_send.at[place - 1, h], slot_recv.at[place - 1, h], target)

    def to_w(h):
        return fetch(0, 1, h, along_w)

    def to_h(h):
        return fetch(0, 2, h, along_h)

    def to_relay(h):
        return fetch(2, 3, h, relay)

    def to_y(h):
        return fetch(3, 4, h, below)

    def part_copy(place, h):
        return remote(
            part_out.at[place, h], part_in.at[place, h], part_send.at[place, h], part_recv.at[place, h], owners[place - 1]
        )

    def final_copy(place, h):
        return remote(
            final_out.at[place, h], final_in.at[place, h], final_send.at[place, h], final_recv.at[place, h], owners[place - 1]
        )

    def ret_copy(place, h, target):
        return remote(
            dq_out.at[place, h], ret_in.at[place, h], ret_send.at[place, h], ret_recv.at[place, h], target
        )

    def ret_w(h):
        return ret_copy(0, h, along_w)

    def ret_h(h):
        return ret_copy(1, h, along_h)

    def ret_relay(h):
        return ret_copy(2, h, relay)

    def ret_y(h):
        return ret_copy(3, h, above)

    flags = []
    for owner in owners:
        hit = jnp.int32(0)
        for entry in range(1, 3):
            same = jnp.where(lists[entry, 0, mine] == owner, 1, 0)
            hit = hit + jnp.where(entry < counts[mine], same, 0)
        flags.append(hit > 0)

    def stats(place, h):
        query, grad = slots[place, h, 0], slots[place, h, 1]
        top = total = inner = None
        for block in range(ROWS // BLOCK):
            rows = pl.ds(block * BLOCK, BLOCK)
            scores = dot_t(keys[h, 0, rows], query) * scale2
            dprob = dot_t(keys[h, 1, rows], grad)
            high = jnp.max(scores, axis=0, keepdims=True)
            new_top = high if top is None else jnp.maximum(top, high)
            weight = jnp.exp2(scores - new_top)
            new_total = jnp.sum(weight, axis=0, keepdims=True)
            new_inner = jnp.sum(weight * dprob, axis=0, keepdims=True)
            if top is not None:
                keep = jnp.exp2(top - new_top)
                new_total = new_total + total * keep
                new_inner = new_inner + inner * keep
            top, total, inner = new_top, new_total, new_inner
        part_out[place, h] = stacked(top + jnp.log(total) * LOG2E, inner / total)

    def combine(h):
        parts = [part_out[0, h]] + [part_in[n + 1, h] for n in range(NEAR)]
        tops = [parts[0][0:1]] + [jnp.where(flags[n], parts[n + 1][0:1], -FAR) for n in range(NEAR)]
        top = functools.reduce(jnp.maximum, tops)
        weights = [jnp.exp2(t - top) for t in tops]
        total = sum(weights)
        log_total = top + jnp.log(total) * LOG2E
        delta = sum(p[1:2] * w for p, w in zip(parts, weights)) / total
        final_in[0, h] = stacked(log_total, delta)
        for n in range(NEAR):
            final_out[n + 1, h] = stacked(jnp.where(flags[n], log_total, FAR), delta)

    def grads(place, h):
        query, grad = slots[place, h, 0], slots[place, h, 1]
        final = final_in[place, h]
        log_total, delta = final[0:1], final[1:2]
        for block in range(ROWS // BLOCK):
            rows = pl.ds(block * BLOCK, BLOCK)
            scores = dot_t(keys[h, 0, rows], query) * scale2
            dprob = dot_t(keys[h, 1, rows], grad)
            prob = jnp.exp2(scores - log_total)
            dscore = (prob * (dprob - delta)).astype(BF16)
            ds_ref[rows] = dscore
            dv_acc[rows] += dot(prob.astype(BF16), grad)
            dk_acc[rows] += dot(dscore, query)
        dq32[place, h] = dot(key_t[h], ds_ref[...]) * factor

    def norm_backward(grad, raw, gain):
        wide = raw.astype(F32)
        inverse = inverse_norm(wide)
        normed = wide * inverse
        scaled = grad * gain
        mean = jnp.mean(normed * scaled, axis=-1, keepdims=True)
        return ((scaled - normed * mean) * inverse).astype(BF16), jnp.sum(grad * normed, axis=0, keepdims=True)

    def backward(h):
        dk_acc[...] = jnp.zeros_like(dk_acc)
        dv_acc[...] = jnp.zeros_like(dv_acc)

        def one(index, carry):
            place = NEAR - index
            grads(place, h)

            @pl.when(place == 4)
            def _():
                dq_out[3, h] = dq32[4, h].astype(BF16)
                ret_y(h).start()

            @pl.when(place == 1)
            def _():
                dq_out[0, h] = dq32[1, h].astype(BF16)
                ret_w(h).start()

            return carry

        lax.fori_loop(0, NEAR + 1, one, 0)

    def finish_k(h):
        grads_ref[2, :, lanes(h)] = dv_acc[...].astype(BF16)
        grad_key = dk_acc[...] * factor
        grad, gain = norm_backward(grad_key, k_ref[:, lanes(h)], gain_k_ref[...])
        grads_ref[1, :, lanes(h)] = grad
        paired = jnp.sum(grad_key * keys[h, 0].astype(F32), axis=0, keepdims=True) / gain_q_ref[...]
        gain_ref[...] += stacked(paired, gain)

    def finish_q(h):
        total = dq32[0, h] + ret_in[0, h].astype(F32) + ret_in[1, h].astype(F32)
        grad, _ = norm_backward(total.T, q_ref[:, lanes(h)], gain_q_ref[...])
        grads_ref[0, :, lanes(h)] = grad

    def gain_copies(g):
        held, me, where = groups[g]
        return [
            pltpu.make_async_remote_copy(
                src_ref=held.at[me], dst_ref=held.at[me], send_sem=gain_send.at[g, hop], recv_sem=gain_recv.at[g, hop],
                device_id=where((me + hop) % RING), device_id_type=MESH,
            )
            for hop in range(1, RING)
        ]

    def gain_start(g, value):
        held, me, _ = groups[g]
        held[me] = value
        for copy in gain_copies(g):
            copy.start()

    def gain_finish(g):
        held, _, _ = groups[g]
        for copy in gain_copies(g):
            copy.wait_recv()
        value = held[0]
        for place in range(1, RING):
            value = value + held[place]
        return value

    gain_ref[...] = jnp.zeros_like(gain_ref)
    lax.fori_loop(0, HEADS_HERE, prepare_q, 0)
    pl.semaphore_wait(barrier, 7 + 3 * (RING - 1))
    to_h(0).start()
    to_w(0).start()
    to_h(1).start()
    to_h(2).start()
    lax.fori_loop(0, HEADS_HERE, prepare_k, 0)

    last = HEADS_HERE + 3

    def step(i, carry):
        def on(lag, stage):
            h = i - lag

            @pl.when(jnp.logical_and(h >= 0, h < HEADS_HERE))
            def _():
                stage(h)

        def arrive(h):
            to_h(h).wait_recv()
            to_relay(h).start()

            @pl.when(h + 3 < HEADS_HERE)
            def _():
                to_h(h + 3).start()

            @pl.when(h + 1 < HEADS_HERE)
            def _():
                to_w(h + 1).start()

            stats(0, h)
            stats(2, h)

        def pass_on(h):
            to_relay(h).wait_recv()
            to_y(h).start()

        def near_w(h):
            to_w(h).wait_recv()
            stats(1, h)

        def send_parts(h):
            to_y(h).wait_recv()
            stats(4, h)
            for place in range(1, NEAR + 1):
                part_copy(place, h).start()

        def pairs(h):
            for place in range(1, NEAR + 1):
                final_copy(place, h).wait_recv()
            backward(h)
            finish_k(h)

        def send_finals(h):
            for place in range(1, NEAR + 1):
                part_copy(place, h).wait_recv()
            combine(h)
            for place in range(1, NEAR + 1):
                final_copy(place, h).start()

        def back_y(h):
            ret_y(h).wait_recv()
            dq_out[2, h] = (dq32[3, h] + ret_in[3, h].astype(F32)).astype(BF16)
            ret_relay(h).start()

        def back_relay(h):
            ret_relay(h).wait_recv()
            dq_out[1, h] = (dq32[2, h] + ret_in[2, h].astype(F32)).astype(BF16)
            ret_h(h).start()

        def back_home(h):
            ret_w(h).wait_recv()
            ret_h(h).wait_recv()
            finish_q(h)

        on(0, arrive)
        on(1, pass_on)
        on(0, near_w)
        on(1, lambda h: stats(3, h))
        on(3, send_finals)
        on(2, send_parts)
        on(6, back_relay)
        on(5, back_y)
        on(4, pairs)
        pl.when(i == last)(lambda: gain_start(0, gain_ref[...]))
        on(7, back_home)
        pl.when(i == last + 1)(lambda: gain_start(1, gain_finish(0)))
        pl.when(i == last + 2)(lambda: gain_start(2, gain_finish(1)))
        return carry

    lax.fori_loop(0, HEADS_HERE + 7, step, 0)
    gains = gain_finish(2) * (4 * 64 * ROWS) ** (-0.5)
    gain_q_out[...] = gains[0:1]
    gain_k_out[...] = gains[1:2]

    def drain(h, carry):
        for copy in (to_w, to_h, to_relay, to_y, ret_w, ret_h, ret_relay, ret_y):
            copy(h).wait_send()
        for place in range(1, NEAR + 1):
            part_copy(place, h).wait_send()
            final_copy(place, h).wait_send()
        return carry

    lax.fori_loop(0, HEADS_HERE, drain, 0)
    for g in range(3):
        for copy in gain_copies(g):
            copy.wait_send()


def attention(lists, counts, q, k, v, g, gain_q, gain_k):
    n = HEADS_HERE
    vmem = pl.BlockSpec(memory_space=pltpu.VMEM)
    smem = pl.BlockSpec(memory_space=pltpu.SMEM)
    big = jax.ShapeDtypeStruct((3, ROWS, n * HD), BF16)
    gain = jax.ShapeDtypeStruct((1, HD), F32)
    sem = pltpu.SemaphoreType.DMA
    return pl.pallas_call(
        attention_kernel,
        name="tile_attention",
        out_shape=(big, gain, gain),
        in_specs=[smem, smem] + [vmem] * 6,
        out_specs=(vmem,) * 3,
        scratch_shapes=[
            pltpu.VMEM((5, n, 2, ROWS, HD), BF16),
            pltpu.VMEM((n, 2, ROWS, HD), BF16),
            pltpu.VMEM((n, HD, ROWS), BF16),
            pltpu.VMEM((5, n, 2, ROWS), F32),
            pltpu.VMEM((5, n, 2, ROWS), F32),
            pltpu.VMEM((5, n, 2, ROWS), F32),
            pltpu.VMEM((5, n, 2, ROWS), F32),
            pltpu.VMEM((5, n, HD, ROWS), F32),
            pltpu.VMEM((4, n, HD, ROWS), BF16),
            pltpu.VMEM((4, n, HD, ROWS), BF16),
            pltpu.VMEM((ROWS, ROWS), BF16),
            pltpu.VMEM((ROWS, HD), F32),
            pltpu.VMEM((ROWS, HD), F32),
            pltpu.VMEM((2, HD), F32),
            pltpu.VMEM((RING, 2, HD), F32),
            pltpu.VMEM((RING, 2, HD), F32),
            pltpu.VMEM((RING, 2, HD), F32),
            sem((4, n)), sem((4, n)), sem((5, n)), sem((5, n)), sem((5, n)), sem((5, n)), sem((4, n)), sem((4, n)),
            sem((3, RING)), sem((3, RING)),
        ],
        compiler_params=pltpu.CompilerParams(collective_id=1, has_side_effects=True, vmem_limit_bytes=56 * 2**20),
    )(lists, counts, q, k, v, g, gain_q, gain_k)


def shards(q_raw, k_raw, values, d_out, gain_q, gain_k, tile_lists, tile_counts):
    grads, total_q, total_k = attention(
        jnp.transpose(tile_lists, (2, 0, 1)), tile_counts[0], q_raw[0], k_raw[0], values[0], d_out[0],
        gain_q[None], gain_k[None],
    )
    return (grads[0:1], grads[1:2], grads[2:3], total_q[0], total_k[0])


def solution(mesh):
    split = P("dp", "seq", "tensor")
    return jax.shard_map(
        shards,
        mesh=mesh,
        in_specs=(split, split, split, split, P(), P(), P("dp", None, None), P("dp", None)),
        out_specs=(split, split, split, P(), P()),
        check_vma=False,
    )
```

```python
import functools

import jax
import jax.numpy as jnp
from jax import lax
from jax.experimental import pallas as pl
from jax.experimental.pallas import tpu as pltpu
from jax.sharding import PartitionSpec as P

MESH = pl.DeviceIdType.MESH
EPS = 1e-06
LOG2E = 1.4426950408889634
FAR = 1e30
ROWS = 384
HD = 128
HEADS_HERE = 6
BLOCK = 128
RING = 8
NEAR = 4
F32 = jnp.float32
BF16 = jnp.bfloat16


def flip(z, mask):
    result = z
    for bit in (1, 2, 4):
        if mask & bit:
            result = result + bit - 2 * bit * ((z // bit) % 2)
    return result


def dot_t(a, b):
    return lax.dot_general(a, b, (((1,), (1,)), ((), ())), preferred_element_type=F32)


def dot(a, b):
    return lax.dot_general(a, b, (((1,), (0,)), ((), ())), preferred_element_type=F32)


def inverse_norm(wide):
    return lax.rsqrt(jnp.mean(wide * wide, axis=-1, keepdims=True) + EPS)


def stacked(first, second):
    place = lax.broadcasted_iota(jnp.int32, (2, first.shape[-1]), 0)
    return jnp.where(place == 0, first, second)


def attention_kernel(
    lists, counts, q_hbm, k_hbm, v_hbm, g_hbm, gain_q_ref, gain_k_ref,
    grads_ref, gain_q_out, gain_k_out,
    slots, keys, key_t, part_out, part_in, final_out, final_in, dq32, dq_out, ret_in, ds_ref, dk_acc, dv_acc,
    gain_ref, gain_a, gain_b, gain_c, q_ref, k_ref,
    slot_send, slot_recv, part_send, part_recv, final_send, final_recv, ret_send, ret_recv, gain_send, gain_recv, load_sem,
):
    factor = HD ** (-0.5)
    scale2 = factor * LOG2E
    mine = lax.axis_index("seq")
    y, z = mine // RING, mine % RING
    late = z // 4
    y_next = (y + 1 - 2 * late + RING) % RING
    y_prev = (y - 1 + 2 * late + RING) % RING
    along_w = y * RING + flip(z, 1)
    along_h = y * RING + flip(z, 2)
    relay = y * RING + flip(z, 6)
    along_t = y * RING + flip(z, 4)
    along_u = y_prev * RING + flip(z, 4)
    below = y_next * RING + z
    above = y_prev * RING + z
    owners = (along_w, along_h, along_t, along_u)

    barrier = pltpu.get_barrier_semaphore()
    for partner in (along_w, along_h, relay, along_t, along_u, below, above):
        pl.semaphore_signal(barrier, inc=1, device_id={"seq": partner}, device_id_type=MESH)
    clip, core = lax.axis_index("dp"), lax.axis_index("tensor")
    groups = (
        (gain_a, clip * 2 + core, lambda p: {"dp": p // 2, "tensor": p % 2}),
        (gain_b, y, lambda p: {"seq": p * RING + z}),
        (gain_c, z, lambda p: {"seq": y * RING + p}),
    )
    for _, me, where in groups:
        for hop in range(1, RING):
            pl.semaphore_signal(barrier, inc=1, device_id=where((me + hop) % RING), device_id_type=MESH)

    def lanes(h):
        return pl.ds(pl.multiple_of(h * HD, HD), HD)

    def load_g(h):
        return pltpu.make_async_copy(g_hbm.at[:, lanes(h)], slots.at[0, h, 1], load_sem.at[0, h])

    def load_v(h):
        return pltpu.make_async_copy(v_hbm.at[:, lanes(h)], keys.at[h, 1], load_sem.at[1, h])

    load_q = pltpu.make_async_copy(q_hbm, q_ref, load_sem.at[2, 0])
    load_k = pltpu.make_async_copy(k_hbm, k_ref, load_sem.at[2, 1])
    load_q.start()
    for h in range(HEADS_HERE):
        load_g(h).start()
    load_k.start()
    for h in range(HEADS_HERE):
        load_v(h).start()

    def prepare_q(h, carry):
        wide = q_ref[:, lanes(h)].astype(F32)
        slots[0, h, 0] = (wide * inverse_norm(wide) * gain_q_ref[...]).astype(BF16)
        return carry

    def prepare_k(h, carry):
        wide = k_ref[:, lanes(h)].astype(F32)
        key = (wide * inverse_norm(wide) * gain_k_ref[...]).astype(BF16)
        keys[h, 0] = key
        key_t[h] = key.astype(F32).T.astype(BF16)
        return carry

    def remote(src, dst, send, recv, target):
        return pltpu.make_async_remote_copy(
            src_ref=src, dst_ref=dst, send_sem=send, recv_sem=recv, device_id={"seq": target}, device_id_type=MESH
        )

    def fetch(source, place, h, target):
        return remote(slots.at[source, h], slots.at[place, h], slot_send.at[place - 1, h], slot_recv.at[place - 1, h], target)

    def to_w(h):
        return fetch(0, 1, h, along_w)

    def to_h(h):
        return fetch(0, 2, h, along_h)

    def to_relay(h):
        return fetch(2, 3, h, relay)

    def to_y(h):
        return fetch(3, 4, h, below)

    def part_copy(place, h):
        return remote(
            part_out.at[place, h], part_in.at[place, h], part_send.at[place, h], part_recv.at[place, h], owners[place - 1]
        )

    def final_copy(place, h):
        return remote(
            final_out.at[place, h], final_in.at[place, h], final_send.at[place, h], final_recv.at[place, h], owners[place - 1]
        )

    def ret_copy(place, h, target):
        return remote(
            dq_out.at[place, h], ret_in.at[place, h], ret_send.at[place, h], ret_recv.at[place, h], target
        )

    def ret_w(h):
        return ret_copy(0, h, along_w)

    def ret_h(h):
        return ret_copy(1, h, along_h)

    def ret_relay(h):
        return ret_copy(2, h, relay)

    def ret_y(h):
        return ret_copy(3, h, above)

    flags = []
    for owner in owners:
        hit = jnp.int32(0)
        for entry in range(1, 3):
            same = jnp.where(lists[entry, 0, mine] == owner, 1, 0)
            hit = hit + jnp.where(entry < counts[mine], same, 0)
        flags.append(hit > 0)

    def stats(place, h):
        query, grad = slots[place, h, 0], slots[place, h, 1]
        top = total = inner = None
        for block in range(ROWS // BLOCK):
            rows = pl.ds(block * BLOCK, BLOCK)
            scores = dot_t(keys[h, 0, rows], query) * scale2
            dprob = dot_t(keys[h, 1, rows], grad)
            high = jnp.max(scores, axis=0, keepdims=True)
            new_top = high if top is None else jnp.maximum(top, high)
            weight = jnp.exp2(scores - new_top)
            new_total = jnp.sum(weight, axis=0, keepdims=True)
            new_inner = jnp.sum(weight * dprob, axis=0, keepdims=True)
            if top is not None:
                keep = jnp.exp2(top - new_top)
                new_total = new_total + total * keep
                new_inner = new_inner + inner * keep
            top, total, inner = new_top, new_total, new_inner
        part_out[place, h] = stacked(top + jnp.log(total) * LOG2E, inner / total)

    def combine(h):
        parts = [part_out[0, h]] + [part_in[n + 1, h] for n in range(NEAR)]
        tops = [parts[0][0:1]] + [jnp.where(flags[n], parts[n + 1][0:1], -FAR) for n in range(NEAR)]
        top = functools.reduce(jnp.maximum, tops)
        weights = [jnp.exp2(t - top) for t in tops]
        total = sum(weights)
        log_total = top + jnp.log(total) * LOG2E
        delta = sum(p[1:2] * w for p, w in zip(parts, weights)) / total
        final_in[0, h] = stacked(log_total, delta)
        for n in range(NEAR):
            final_out[n + 1, h] = stacked(jnp.where(flags[n], log_total, FAR), delta)

    def grads(place, h):
        query, grad = slots[place, h, 0], slots[place, h, 1]
        final = final_in[place, h]
        log_total, delta = final[0:1], final[1:2]
        for block in range(ROWS // BLOCK):
            rows = pl.ds(block * BLOCK, BLOCK)
            scores = dot_t(keys[h, 0, rows], query) * scale2
            dprob = dot_t(keys[h, 1, rows], grad)
            prob = jnp.exp2(scores - log_total)
            dscore = (prob * (dprob - delta)).astype(BF16)
            ds_ref[rows] = dscore
            dv_acc[rows] += dot(prob.astype(BF16), grad)
            dk_acc[rows] += dot(dscore, query)
        dq32[place, h] = dot(key_t[h], ds_ref[...]) * factor

    def norm_backward(grad, raw, gain):
        wide = raw.astype(F32)
        inverse = inverse_norm(wide)
        normed = wide * inverse
        scaled = grad * gain
        mean = jnp.mean(normed * scaled, axis=-1, keepdims=True)
        return ((scaled - normed * mean) * inverse).astype(BF16), jnp.sum(grad * normed, axis=0, keepdims=True)

    def backward(h):
        dk_acc[...] = jnp.zeros_like(dk_acc)
        dv_acc[...] = jnp.zeros_like(dv_acc)

        def one(index, carry):
            place = NEAR - index
            grads(place, h)

            @pl.when(place == 4)
            def _():
                dq_out[3, h] = dq32[4, h].astype(BF16)
                ret_y(h).start()

            @pl.when(place == 1)
            def _():
                dq_out[0, h] = dq32[1, h].astype(BF16)
                ret_w(h).start()

            return carry

        lax.fori_loop(0, NEAR + 1, one, 0)

    def finish_k(h):
        grads_ref[2, :, lanes(h)] = dv_acc[...].astype(BF16)
        grad_key = dk_acc[...] * factor
        grad, gain = norm_backward(grad_key, k_ref[:, lanes(h)], gain_k_ref[...])
        grads_ref[1, :, lanes(h)] = grad
        paired = jnp.sum(grad_key * keys[h, 0].astype(F32), axis=0, keepdims=True) / gain_q_ref[...]
        gain_ref[...] += stacked(paired, gain)

    def finish_q(h):
        total = dq32[0, h] + ret_in[0, h].astype(F32) + ret_in[1, h].astype(F32)
        grad, _ = norm_backward(total.T, q_ref[:, lanes(h)], gain_q_ref[...])
        grads_ref[0, :, lanes(h)] = grad

    def gain_copies(g):
        held, me, where = groups[g]
        return [
            pltpu.make_async_remote_copy(
                src_ref=held.at[me], dst_ref=held.at[me], send_sem=gain_send.at[g, hop], recv_sem=gain_recv.at[g, hop],
                device_id=where((me + hop) % RING), device_id_type=MESH,
            )
            for hop in range(1, RING)
        ]

    def gain_start(g, value):
        held, me, _ = groups[g]
        held[me] = value
        for copy in gain_copies(g):
            copy.start()

    def gain_finish(g):
        held, _, _ = groups[g]
        for copy in gain_copies(g):
            copy.wait_recv()
        value = held[0]
        for place in range(1, RING):
            value = value + held[place]
        return value

    gain_ref[...] = jnp.zeros_like(gain_ref)
    load_q.wait()
    for h in range(3):
        prepare_q(h, 0)
        load_g(h).wait()
        if h == 0:
            pl.semaphore_wait(barrier, 7 + 3 * (RING - 1))
            to_w(h).start()
        to_h(h).start()
    lax.fori_loop(3, HEADS_HERE, prepare_q, 0)
    for h in range(3, HEADS_HERE):
        load_g(h).wait()
    load_k.wait()
    lax.fori_loop(0, HEADS_HERE, prepare_k, 0)
    for h in range(HEADS_HERE):
        load_v(h).wait()

    last = HEADS_HERE + 3

    def step(i, carry):
        def on(lag, stage):
            h = i - lag

            @pl.when(jnp.logical_and(h >= 0, h < HEADS_HERE))
            def _():
                stage(h)

        def arrive(h):
            to_h(h).wait_recv()
            to_relay(h).start()

            @pl.when(h + 3 < HEADS_HERE)
            def _():
                to_h(h + 3).start()

            @pl.when(h + 1 < HEADS_HERE)
            def _():
                to_w(h + 1).start()

            stats(0, h)
            stats(2, h)

        def pass_on(h):
            to_relay(h).wait_recv()
            to_y(h).start()

        def near_w(h):
            to_w(h).wait_recv()
            stats(1, h)

        def send_parts(h):
            to_y(h).wait_recv()
            stats(4, h)
            for place in range(1, NEAR + 1):
                part_copy(place, h).start()

        def pairs(h):
            for place in range(1, NEAR + 1):
                final_copy(place, h).wait_recv()
            backward(h)
            finish_k(h)

        def send_finals(h):
            for place in range(1, NEAR + 1):
                part_copy(place, h).wait_recv()
            combine(h)
            for place in range(1, NEAR + 1):
                final_copy(place, h).start()

        def back_y(h):
            ret_y(h).wait_recv()
            dq_out[2, h] = (dq32[3, h] + ret_in[3, h].astype(F32)).astype(BF16)
            ret_relay(h).start()

        def back_relay(h):
            ret_relay(h).wait_recv()
            dq_out[1, h] = (dq32[2, h] + ret_in[2, h].astype(F32)).astype(BF16)
            ret_h(h).start()

        def back_home(h):
            ret_w(h).wait_recv()
            ret_h(h).wait_recv()
            finish_q(h)

        on(0, arrive)
        on(1, pass_on)
        on(0, near_w)
        on(1, lambda h: stats(3, h))
        on(3, send_finals)
        on(2, send_parts)
        on(6, back_relay)
        pl.when(i == last + 2)(lambda: gain_start(2, gain_finish(1)))
        on(5, back_y)
        pl.when(i == last + 1)(lambda: gain_start(1, gain_finish(0)))
        on(4, pairs)
        pl.when(i == last)(lambda: gain_start(0, gain_ref[...]))
        on(7, back_home)
        return carry

    lax.fori_loop(0, HEADS_HERE + 7, step, 0)
    gains = gain_finish(2) * (4 * 64 * ROWS) ** (-0.5)
    gain_q_out[...] = gains[0:1]
    gain_k_out[...] = gains[1:2]

    def drain(h, carry):
        for copy in (to_w, to_h, to_relay, to_y, ret_w, ret_h, ret_relay, ret_y):
            copy(h).wait_send()
        for place in range(1, NEAR + 1):
            part_copy(place, h).wait_send()
            final_copy(place, h).wait_send()
        return carry

    lax.fori_loop(0, HEADS_HERE, drain, 0)
    for g in range(3):
        for copy in gain_copies(g):
            copy.wait_send()


def attention(lists, counts, q, k, v, g, gain_q, gain_k):
    n = HEADS_HERE
    vmem = pl.BlockSpec(memory_space=pltpu.VMEM)
    smem = pl.BlockSpec(memory_space=pltpu.SMEM)
    hbm = pl.BlockSpec(memory_space=pltpu.HBM)
    big = jax.ShapeDtypeStruct((3, ROWS, n * HD), BF16)
    gain = jax.ShapeDtypeStruct((1, HD), F32)
    sem = pltpu.SemaphoreType.DMA
    return pl.pallas_call(
        attention_kernel,
        name="tile_attention",
        out_shape=(big, gain, gain),
        in_specs=[smem, smem] + [hbm] * 4 + [vmem] * 2,
        out_specs=(vmem,) * 3,
        scratch_shapes=[
            pltpu.VMEM((5, n, 2, ROWS, HD), BF16),
            pltpu.VMEM((n, 2, ROWS, HD), BF16),
            pltpu.VMEM((n, HD, ROWS), BF16),
            pltpu.VMEM((5, n, 2, ROWS), F32),
            pltpu.VMEM((5, n, 2, ROWS), F32),
            pltpu.VMEM((5, n, 2, ROWS), F32),
            pltpu.VMEM((5, n, 2, ROWS), F32),
            pltpu.VMEM((5, n, HD, ROWS), F32),
            pltpu.VMEM((4, n, HD, ROWS), BF16),
            pltpu.VMEM((4, n, HD, ROWS), BF16),
            pltpu.VMEM((ROWS, ROWS), BF16),
            pltpu.VMEM((ROWS, HD), F32),
            pltpu.VMEM((ROWS, HD), F32),
            pltpu.VMEM((2, HD), F32),
            pltpu.VMEM((RING, 2, HD), F32),
            pltpu.VMEM((RING, 2, HD), F32),
            pltpu.VMEM((RING, 2, HD), F32),
            pltpu.VMEM((ROWS, n * HD), BF16),
            pltpu.VMEM((ROWS, n * HD), BF16),
            sem((4, n)), sem((4, n)), sem((5, n)), sem((5, n)), sem((5, n)), sem((5, n)), sem((4, n)), sem((4, n)),
            sem((3, RING)), sem((3, RING)), sem((3, n)),
        ],
        compiler_params=pltpu.CompilerParams(collective_id=1, has_side_effects=True, vmem_limit_bytes=56 * 2**20),
    )(lists, counts, q, k, v, g, gain_q, gain_k)


def shards(q_raw, k_raw, values, d_out, gain_q, gain_k, tile_lists, tile_counts):
    grads, total_q, total_k = attention(
        jnp.transpose(tile_lists, (2, 0, 1)), tile_counts[0], q_raw[0], k_raw[0], values[0], d_out[0],
        gain_q[None], gain_k[None],
    )
    return (grads[0:1], grads[1:2], grads[2:3], total_q[0], total_k[0])


def solution(mesh):
    split = P("dp", "seq", "tensor")
    return jax.shard_map(
        shards,
        mesh=mesh,
        in_specs=(split, split, split, split, P(), P(), P("dp", None, None), P("dp", None)),
        out_specs=(split, split, split, P(), P()),
        check_vma=False,
    )
```

```python
import functools

import jax
import jax.numpy as jnp
from jax import lax
from jax.experimental import pallas as pl
from jax.experimental.pallas import tpu as pltpu
from jax.sharding import PartitionSpec as P

MESH = pl.DeviceIdType.MESH
EPS = 1e-06
LOG2E = 1.4426950408889634
FAR = 1e30
ROWS = 384
HD = 128
HEADS_HERE = 6
BLOCK = 128
RING = 8
NEAR = 4
F32 = jnp.float32
BF16 = jnp.bfloat16


def flip(z, mask):
    result = z
    for bit in (1, 2, 4):
        if mask & bit:
            result = result + bit - 2 * bit * ((z // bit) % 2)
    return result


def dot_t(a, b):
    return lax.dot_general(a, b, (((1,), (1,)), ((), ())), preferred_element_type=F32)


def dot(a, b):
    return lax.dot_general(a, b, (((1,), (0,)), ((), ())), preferred_element_type=F32)


def inverse_norm(wide):
    return lax.rsqrt(jnp.mean(wide * wide, axis=-1, keepdims=True) + EPS)


def stacked(first, second):
    place = lax.broadcasted_iota(jnp.int32, (2, first.shape[-1]), 0)
    return jnp.where(place == 0, first, second)


def attention_kernel(
    lists, counts, q_hbm, k_hbm, v_hbm, g_hbm, gain_q_ref, gain_k_ref,
    grads_ref, gain_q_out, gain_k_out,
    slots, keys, key_t, part_out, part_in, final_out, final_in, dq32, dq_out, ret_in, ds_ref, dk_acc, dv_acc,
    gain_ref, gain_a, gain_b, gain_c, q_ref, k_ref,
    slot_send, slot_recv, part_send, part_recv, final_send, final_recv, ret_send, ret_recv, gain_send, gain_recv, load_sem,
):
    factor = HD ** (-0.5)
    scale2 = factor * LOG2E
    mine = lax.axis_index("seq")
    y, z = mine // RING, mine % RING
    late = z // 4
    y_next = (y + 1 - 2 * late + RING) % RING
    y_prev = (y - 1 + 2 * late + RING) % RING
    along_w = y * RING + flip(z, 1)
    along_h = y * RING + flip(z, 2)
    relay = y * RING + flip(z, 6)
    along_t = y * RING + flip(z, 4)
    along_u = y_prev * RING + flip(z, 4)
    below = y_next * RING + z
    above = y_prev * RING + z
    owners = (along_w, along_h, along_t, along_u)

    barrier = pltpu.get_barrier_semaphore()
    for partner in (along_w, along_h, relay, along_t, along_u, below, above):
        pl.semaphore_signal(barrier, inc=1, device_id={"seq": partner}, device_id_type=MESH)
    clip, core = lax.axis_index("dp"), lax.axis_index("tensor")
    groups = (
        (gain_a, clip * 2 + core, lambda p: {"dp": p // 2, "tensor": p % 2}),
        (gain_b, y, lambda p: {"seq": p * RING + z}),
        (gain_c, z, lambda p: {"seq": y * RING + p}),
    )
    for _, me, where in groups:
        for hop in range(1, RING):
            pl.semaphore_signal(barrier, inc=1, device_id=where((me + hop) % RING), device_id_type=MESH)

    def lanes(h):
        return pl.ds(pl.multiple_of(h * HD, HD), HD)

    def load_g(h):
        return pltpu.make_async_copy(g_hbm.at[:, lanes(h)], slots.at[0, h, 1], load_sem.at[0, h])

    def load_v(h):
        return pltpu.make_async_copy(v_hbm.at[:, lanes(h)], keys.at[h, 1], load_sem.at[1, h])

    load_q = pltpu.make_async_copy(q_hbm, q_ref, load_sem.at[2, 0])
    load_k = pltpu.make_async_copy(k_hbm, k_ref, load_sem.at[2, 1])
    load_q.start()
    for h in range(HEADS_HERE):
        load_g(h).start()
    load_k.start()
    for h in range(HEADS_HERE):
        load_v(h).start()

    def prepare_q(h, carry):
        wide = q_ref[:, lanes(h)].astype(F32)
        slots[0, h, 0] = (wide * inverse_norm(wide) * gain_q_ref[...]).astype(BF16)
        return carry

    def prepare_k(h, carry):
        wide = k_ref[:, lanes(h)].astype(F32)
        key = (wide * inverse_norm(wide) * gain_k_ref[...]).astype(BF16)
        keys[h, 0] = key
        key_t[h] = key.astype(F32).T.astype(BF16)
        return carry

    def remote(src, dst, send, recv, target):
        return pltpu.make_async_remote_copy(
            src_ref=src, dst_ref=dst, send_sem=send, recv_sem=recv, device_id={"seq": target}, device_id_type=MESH
        )

    def fetch(source, place, h, target):
        return remote(slots.at[source, h], slots.at[place, h], slot_send.at[place - 1, h], slot_recv.at[place - 1, h], target)

    def to_w(h):
        return fetch(0, 1, h, along_w)

    def to_h(h):
        return fetch(0, 2, h, along_h)

    def to_relay(h):
        return fetch(2, 3, h, relay)

    def to_y(h):
        return fetch(3, 4, h, below)

    def part_copy(place, h):
        return remote(
            part_out.at[place, h], part_in.at[place, h], part_send.at[place, h], part_recv.at[place, h], owners[place - 1]
        )

    def final_copy(place, h):
        return remote(
            final_out.at[place, h], final_in.at[place, h], final_send.at[place, h], final_recv.at[place, h], owners[place - 1]
        )

    def ret_copy(place, h, target):
        return remote(
            dq_out.at[place, h], ret_in.at[place, h], ret_send.at[place, h], ret_recv.at[place, h], target
        )

    def ret_w(h):
        return ret_copy(0, h, along_w)

    def ret_h(h):
        return ret_copy(1, h, along_h)

    def ret_relay(h):
        return ret_copy(2, h, relay)

    def ret_y(h):
        return ret_copy(3, h, above)

    flags = []
    for owner in owners:
        hit = jnp.int32(0)
        for entry in range(1, 3):
            same = jnp.where(lists[entry, 0, mine] == owner, 1, 0)
            hit = hit + jnp.where(entry < counts[mine], same, 0)
        flags.append(hit > 0)

    def stats(place, h):
        query, grad = slots[place, h, 0], slots[place, h, 1]
        top = total = inner = None
        for block in range(ROWS // BLOCK):
            rows = pl.ds(block * BLOCK, BLOCK)
            scores = dot_t(keys[h, 0, rows], query) * scale2
            dprob = dot_t(keys[h, 1, rows], grad)
            high = jnp.max(scores, axis=0, keepdims=True)
            new_top = high if top is None else jnp.maximum(top, high)
            weight = jnp.exp2(scores - new_top)
            new_total = jnp.sum(weight, axis=0, keepdims=True)
            new_inner = jnp.sum(weight * dprob, axis=0, keepdims=True)
            if top is not None:
                keep = jnp.exp2(top - new_top)
                new_total = new_total + total * keep
                new_inner = new_inner + inner * keep
            top, total, inner = new_top, new_total, new_inner
        part_out[place, h] = stacked(top + jnp.log(total) * LOG2E, inner / total)

    def combine(h):
        parts = [part_out[0, h]] + [part_in[n + 1, h] for n in range(NEAR)]
        tops = [parts[0][0:1]] + [jnp.where(flags[n], parts[n + 1][0:1], -FAR) for n in range(NEAR)]
        top = functools.reduce(jnp.maximum, tops)
        weights = [jnp.exp2(t - top) for t in tops]
        total = sum(weights)
        log_total = top + jnp.log(total) * LOG2E
        delta = sum(p[1:2] * w for p, w in zip(parts, weights)) / total
        final_in[0, h] = stacked(log_total, delta)
        for n in range(NEAR):
            final_out[n + 1, h] = stacked(jnp.where(flags[n], log_total, FAR), delta)

    def grads(place, h):
        query, grad = slots[place, h, 0], slots[place, h, 1]
        final = final_in[place, h]
        log_total, delta = final[0:1], final[1:2]
        for block in range(ROWS // BLOCK):
            rows = pl.ds(block * BLOCK, BLOCK)
            scores = dot_t(keys[h, 0, rows], query) * scale2
            dprob = dot_t(keys[h, 1, rows], grad)
            prob = jnp.exp2(scores - log_total)
            dscore = (prob * (dprob - delta)).astype(BF16)
            ds_ref[rows] = dscore
            dv_acc[rows] += dot(prob.astype(BF16), grad)
            dk_acc[rows] += dot(dscore, query)
        dq32[place, h] = dot(key_t[h], ds_ref[...]) * factor

    def norm_backward(grad, raw, gain):
        wide = raw.astype(F32)
        inverse = inverse_norm(wide)
        normed = wide * inverse
        scaled = grad * gain
        mean = jnp.mean(normed * scaled, axis=-1, keepdims=True)
        return ((scaled - normed * mean) * inverse).astype(BF16), jnp.sum(grad * normed, axis=0, keepdims=True)

    def backward(h):
        dk_acc[...] = jnp.zeros_like(dk_acc)
        dv_acc[...] = jnp.zeros_like(dv_acc)

        def one(index, carry):
            place = NEAR - index
            grads(place, h)

            @pl.when(place == 4)
            def _():
                dq_out[3, h] = dq32[4, h].astype(BF16)
                ret_y(h).start()

            @pl.when(place == 1)
            def _():
                dq_out[0, h] = dq32[1, h].astype(BF16)
                ret_w(h).start()

            return carry

        lax.fori_loop(0, NEAR + 1, one, 0)

    def finish_k(h):
        grads_ref[2, :, lanes(h)] = dv_acc[...].astype(BF16)
        grad_key = dk_acc[...] * factor
        grad, gain = norm_backward(grad_key, k_ref[:, lanes(h)], gain_k_ref[...])
        grads_ref[1, :, lanes(h)] = grad
        paired = jnp.sum(grad_key * keys[h, 0].astype(F32), axis=0, keepdims=True) / gain_q_ref[...]
        gain_ref[...] += stacked(paired, gain)

    def finish_q(h):
        total = dq32[0, h] + ret_in[0, h].astype(F32) + ret_in[1, h].astype(F32)
        grad, _ = norm_backward(total.T, q_ref[:, lanes(h)], gain_q_ref[...])
        grads_ref[0, :, lanes(h)] = grad

    def gain_copies(g):
        held, me, where = groups[g]
        return [
            pltpu.make_async_remote_copy(
                src_ref=held.at[me], dst_ref=held.at[me], send_sem=gain_send.at[g, hop], recv_sem=gain_recv.at[g, hop],
                device_id=where((me + hop) % RING), device_id_type=MESH,
            )
            for hop in range(1, RING)
        ]

    def gain_start(g, value):
        held, me, _ = groups[g]
        held[me] = value
        for copy in gain_copies(g):
            copy.start()

    def gain_finish(g):
        held, _, _ = groups[g]
        for copy in gain_copies(g):
            copy.wait_recv()
        value = held[0]
        for place in range(1, RING):
            value = value + held[place]
        return value

    gain_ref[...] = jnp.zeros_like(gain_ref)
    load_q.wait()
    for h in range(3):
        prepare_q(h, 0)
        load_g(h).wait()
        if h == 0:
            pl.semaphore_wait(barrier, 7 + 3 * (RING - 1))
            to_w(h).start()
        to_h(h).start()
    lax.fori_loop(3, HEADS_HERE, prepare_q, 0)
    for h in range(3, HEADS_HERE):
        load_g(h).wait()
    load_k.wait()
    lax.fori_loop(0, HEADS_HERE, prepare_k, 0)
    for h in range(HEADS_HERE):
        load_v(h).wait()

    last = HEADS_HERE + 3

    def step(i, carry):
        def on(lag, stage):
            h = i - lag

            @pl.when(jnp.logical_and(h >= 0, h < HEADS_HERE))
            def _():
                stage(h)

        def arrive(h):
            to_h(h).wait_recv()
            to_relay(h).start()

            @pl.when(h + 3 < HEADS_HERE)
            def _():
                to_h(h + 3).start()

            @pl.when(h + 1 < HEADS_HERE)
            def _():
                to_w(h + 1).start()

            stats(0, h)
            stats(2, h)
            part_copy(2, h).start()

        def pass_on(h):
            to_relay(h).wait_recv()
            to_y(h).start()

        def near_w(h):
            to_w(h).wait_recv()
            stats(1, h)
            part_copy(1, h).start()

        def far_t(h):
            stats(3, h)
            part_copy(3, h).start()

        def send_parts(h):
            to_y(h).wait_recv()
            stats(4, h)
            part_copy(4, h).start()

        def pairs(h):
            for place in range(1, NEAR + 1):
                final_copy(place, h).wait_recv()
            backward(h)
            finish_k(h)

        def send_finals(h):
            for place in range(1, NEAR + 1):
                part_copy(place, h).wait_recv()
            combine(h)
            for place in range(1, NEAR + 1):
                final_copy(place, h).start()

        def back_y(h):
            ret_y(h).wait_recv()
            dq_out[2, h] = (dq32[3, h] + ret_in[3, h].astype(F32)).astype(BF16)
            ret_relay(h).start()

        def back_relay(h):
            ret_relay(h).wait_recv()
            dq_out[1, h] = (dq32[2, h] + ret_in[2, h].astype(F32)).astype(BF16)
            ret_h(h).start()

        def back_home(h):
            ret_w(h).wait_recv()
            ret_h(h).wait_recv()
            finish_q(h)

        on(0, arrive)
        on(1, pass_on)
        on(0, near_w)
        on(1, far_t)
        on(3, send_finals)
        on(2, send_parts)
        on(6, back_relay)
        pl.when(i == last + 2)(lambda: gain_start(2, gain_finish(1)))
        on(5, back_y)
        pl.when(i == last + 1)(lambda: gain_start(1, gain_finish(0)))
        on(4, pairs)
        pl.when(i == last)(lambda: gain_start(0, gain_ref[...]))
        on(7, back_home)
        return carry

    lax.fori_loop(0, HEADS_HERE + 7, step, 0)
    gains = gain_finish(2) * (4 * 64 * ROWS) ** (-0.5)
    gain_q_out[...] = gains[0:1]
    gain_k_out[...] = gains[1:2]

    def drain(h, carry):
        for copy in (to_w, to_h, to_relay, to_y, ret_w, ret_h, ret_relay, ret_y):
            copy(h).wait_send()
        for place in range(1, NEAR + 1):
            part_copy(place, h).wait_send()
            final_copy(place, h).wait_send()
        return carry

    lax.fori_loop(0, HEADS_HERE, drain, 0)
    for g in range(3):
        for copy in gain_copies(g):
            copy.wait_send()


def attention(lists, counts, q, k, v, g, gain_q, gain_k):
    n = HEADS_HERE
    vmem = pl.BlockSpec(memory_space=pltpu.VMEM)
    smem = pl.BlockSpec(memory_space=pltpu.SMEM)
    hbm = pl.BlockSpec(memory_space=pltpu.HBM)
    big = jax.ShapeDtypeStruct((3, ROWS, n * HD), BF16)
    gain = jax.ShapeDtypeStruct((1, HD), F32)
    sem = pltpu.SemaphoreType.DMA
    return pl.pallas_call(
        attention_kernel,
        name="tile_attention",
        out_shape=(big, gain, gain),
        in_specs=[smem, smem] + [hbm] * 4 + [vmem] * 2,
        out_specs=(vmem,) * 3,
        scratch_shapes=[
            pltpu.VMEM((5, n, 2, ROWS, HD), BF16),
            pltpu.VMEM((n, 2, ROWS, HD), BF16),
            pltpu.VMEM((n, HD, ROWS), BF16),
            pltpu.VMEM((5, n, 2, ROWS), F32),
            pltpu.VMEM((5, n, 2, ROWS), F32),
            pltpu.VMEM((5, n, 2, ROWS), F32),
            pltpu.VMEM((5, n, 2, ROWS), F32),
            pltpu.VMEM((5, n, HD, ROWS), F32),
            pltpu.VMEM((4, n, HD, ROWS), BF16),
            pltpu.VMEM((4, n, HD, ROWS), BF16),
            pltpu.VMEM((ROWS, ROWS), BF16),
            pltpu.VMEM((ROWS, HD), F32),
            pltpu.VMEM((ROWS, HD), F32),
            pltpu.VMEM((2, HD), F32),
            pltpu.VMEM((RING, 2, HD), F32),
            pltpu.VMEM((RING, 2, HD), F32),
            pltpu.VMEM((RING, 2, HD), F32),
            pltpu.VMEM((ROWS, n * HD), BF16),
            pltpu.VMEM((ROWS, n * HD), BF16),
            sem((4, n)), sem((4, n)), sem((5, n)), sem((5, n)), sem((5, n)), sem((5, n)), sem((4, n)), sem((4, n)),
            sem((3, RING)), sem((3, RING)), sem((3, n)),
        ],
        compiler_params=pltpu.CompilerParams(collective_id=1, has_side_effects=True, vmem_limit_bytes=56 * 2**20),
    )(lists, counts, q, k, v, g, gain_q, gain_k)


def shards(q_raw, k_raw, values, d_out, gain_q, gain_k, tile_lists, tile_counts):
    grads, total_q, total_k = attention(
        jnp.transpose(tile_lists, (2, 0, 1)), tile_counts[0], q_raw[0], k_raw[0], values[0], d_out[0],
        gain_q[None], gain_k[None],
    )
    return (grads[0:1], grads[1:2], grads[2:3], total_q[0], total_k[0])


def solution(mesh):
    split = P("dp", "seq", "tensor")
    return jax.shard_map(
        shards,
        mesh=mesh,
        in_specs=(split, split, split, split, P(), P(), P("dp", None, None), P("dp", None)),
        out_specs=(split, split, split, P(), P()),
        check_vma=False,
    )
```
